128 devices in a mesh: slab: 32 (over z, x, core), sub: 4 (over y).
Axes of the slice: x: 4, y: 4, z: 4, core: 2. Of those that a mesh axis runs over, the one named last changes fastest.
Arguments:
- leaves: bfloat16 [65536, 152], P(('slab', 'sub')), may hold values from -6 to 6
- coarse_local: bfloat16 [8192, 152], P(('slab', 'sub')), may hold values from -6 to 6
- m2m: bfloat16 [8, 152, 152], replicated, may hold values from -0.15625 to 0.15625
- m2l: bfloat16 [316, 152, 152], replicated, may hold values from -0.5 to 0.5
- c2e: float32 [152, 152], replicated, may hold values from -0.0625 to 0.0625
- l2l: bfloat16 [8, 152, 152], replicated, may hold values from -0.5 to 0.5
- send_box: int32 [128, 2560], P(('slab', 'sub')), may hold values from -1 to 63, as said below
- pair_box: int32 [525824], P(('slab', 'sub')), may hold values from 0 to 63, as said below
- pair_partner: int32 [525824], P(('slab', 'sub')), may hold values from -1 to 2623, as said below
- pair_op: int32 [525824], P(('slab', 'sub')), may hold values from 0 to 315, as said below
Outputs:
- parent_local: bfloat16 [8192, 152], P(('slab', 'sub'))
- leaf_local: float32 [65536, 152], P(('slab', 'sub'))
The draws below stay inside these ranges and needn't reach their ends.
Inputs may be any that keep to these rules, and one draw needn't show every extreme that they name: `send_box`: row q, column r * 20 + k: the index among device q's own 64 level-6 boxes of the k-th box whose density device r needs, or -1. In each (q, r) the entries other than -1 come first; q = r is all -1. In every draw one device sends 20 boxes to every other device and receives 20 from every other device. `pair_box`: entry r * 4108 + i: the own box, among device r's 64, of slot i of device r's list. `pair_partner`: entry r * 4108 + i: -1 for a padded slot (padded slots may stand anywhere); below 64: another own box of device r; else 64 + q * 20 + k, the slot k that device q fills for device r, which is not -1 in send_box. In every draw one device has no padded slot and another has 2054 of them, and some live slot names the last row of its table. `pair_op`: A device's 4108 entries form 316 aligned runs of 13 equal ids, and every id fills exactly one run of each device. Id 316 - 1 - k is the opposite vector of id k.
All inputs are finite; a program needn't handle non-finite values.
Results may differ from the reference program's by a relative error of at most 0.0075.
Values may be sent and summed in bfloat16 or wider, within the bound.
No kernel may reach another device: no remote copies, remote signals or barrier semaphores. Data moves between devices by JAX's collectives and lax.ppermute only.
A program may use at most 128 MiB of HBM per device.

```python
import jax
import jax.numpy as jnp
from jax import lax

DENS = 152
NOPS = 316
PB = 64
PAIRS_BOX = 64
CAP = 20
LEAD = 300
OPCAP = 13
PAIRS = 4108
PARENTS = 8192
LEAVES = 65536
N_SLAB = 32
N_SUB = 4


def slot_counts(key):
    devices = N_SLAB * N_SUB
    key_one, key_two, key_three = jax.random.split(jax.random.fold_in(key, 7001), 3)
    fullest = jax.random.randint(key_one, (), 0, devices)
    levels = jax.random.randint(key_two, (devices,), 1, 4)
    base_draw = jax.random.randint(key_three, (devices, devices), 0, CAP + 1)
    counts = jnp.minimum(CAP, base_draw * levels[None, :] // 2)
    source = jnp.arange(devices)[:, None]
    target = jnp.arange(devices)[None, :]
    counts = jnp.where((source == fullest) | (target == fullest), CAP, counts)
    counts = jnp.where(source == target, 0, counts)
    return (fullest, counts)


def pair_table(key):
    devices = N_SLAB * N_SUB
    fullest, counts = slot_counts(key)
    keys = jax.random.split(jax.random.fold_in(key, 9001), 7)
    ranked = jnp.arange(devices)
    receiver = jnp.where(fullest == devices - 1, 0, fullest)
    halved = (receiver + 1) % devices
    live_count = jax.random.randint(keys[0], (devices,), PAIRS // 4, PAIRS + 1)
    live_count = jnp.where(ranked == fullest, PAIRS, live_count)
    live_count = jnp.where(ranked == halved, PAIRS - PAIRS // 2, live_count)
    owned = jax.random.randint(keys[1], (devices, PAIRS), 0, PB)
    sender = jax.random.randint(keys[2], (devices, PAIRS), 0, devices)
    slot_pick = jax.random.randint(keys[3], (devices, PAIRS), 0, CAP)
    usable = slot_pick < counts[sender, ranked[:, None]]
    remote = (jax.random.randint(keys[4], (devices, PAIRS), 0, 2) == 1) & usable
    offset = jax.random.randint(keys[5], (devices, PAIRS), 1, PB)
    partner = jnp.where(remote, PB + sender * CAP + slot_pick, (owned + offset) % PB)

    def permute_one(one_key):
        return jax.random.permutation(one_key, PAIRS)
    places = jax.vmap(permute_one)(jax.random.split(keys[6], devices))
    first_slot = (ranked[:, None] == receiver) & (jnp.arange(PAIRS)[None, :] == 0)
    live = (places < live_count[:, None]) | first_slot
    partner = jnp.where(live, partner, -1)
    top_row = PB + devices * CAP - 1
    partner = jnp.where(first_slot, top_row, partner)
    return (owned.reshape(-1).astype(jnp.int32), partner.reshape(-1).astype(jnp.int32))


def draw_send_box(key, part):
    fullest, counts = slot_counts(key)
    key = jax.random.fold_in(key, 3)
    devices = N_SLAB * N_SUB
    picks = jax.random.randint(key, (devices, devices, CAP), 0, PB)
    in_use = jnp.arange(CAP)[None, None, :] < counts[:, :, None]
    return jnp.where(in_use, picks, -1).reshape(devices, devices * CAP).astype(jnp.int32)


def draw_pair_box(key, part):
    owned, partner = pair_table(key)
    return owned


def draw_pair_partner(key, part):
    owned, partner = pair_table(key)
    return partner


def draw_pair_op(key, part):
    key = jax.random.fold_in(key, 5)
    devices = N_SLAB * N_SUB

    def permute_one(one_key):
        return jax.random.permutation(one_key, NOPS)
    perms = jax.vmap(permute_one)(jax.random.split(key, devices))
    runs = jnp.repeat(perms, OPCAP, axis=1)
    return runs.reshape(-1).astype(jnp.int32)


def steps_of(rng, dims, pieces, smallest, largest):
    def one(axis_at, parts):
        steps = jax.random.uniform(jax.random.fold_in(jax.random.fold_in(rng, 6), axis_at), (parts,), jnp.float32, smallest / len(pieces), largest / len(pieces))
        return jnp.repeat(jnp.exp(steps), dims[axis_at] // parts).reshape((-1,) + (1,) * (len(dims) - axis_at - 1))

    factor_of = one(*pieces[0])
    for cut in pieces[1:]:
        factor_of = factor_of * one(*cut)
    return factor_of


def normal_values(rng, dims, deviation, most, shards=(), kind=jnp.bfloat16):
    drawn = jax.random.normal(rng, dims, jnp.float32) * deviation
    if len(shards) > 0:
        drawn = steps_of(rng, dims, shards, -0.22, 0.18) * drawn
    return jnp.clip(drawn, min=-most, max=most).astype(kind)


def setup_inputs(seed: int = 0) -> dict:
    arg_keys = jax.random.split(jax.random.key(seed), 11)
    leaves = normal_values(arg_keys[0], (LEAVES, DENS), 1.0, 6.0, ((0, 128),))
    coarse_local = normal_values(arg_keys[1], (PARENTS, DENS), 1.0, 6.0, ((0, 128),))
    m2m = normal_values(arg_keys[2], (8, DENS, DENS), (8 * DENS) ** -0.5, 0.15625)
    m2l = normal_values(arg_keys[3], (NOPS, DENS, DENS), DENS ** -0.5, 0.5)
    c2e = normal_values(arg_keys[4], (DENS, DENS), (DENS * PAIRS_BOX) ** -0.5, 0.0625, (), jnp.float32)
    l2l = normal_values(arg_keys[5], (8, DENS, DENS), DENS ** -0.5, 0.5)
    send_box = draw_send_box(jax.random.fold_in(arg_keys[10], 71), 0)
    pair_box = draw_pair_box(jax.random.fold_in(arg_keys[10], 71), 0)
    pair_partner = draw_pair_partner(jax.random.fold_in(arg_keys[10], 71), 0)
    pair_op = draw_pair_op(jax.random.fold_in(arg_keys[10], 71), 0)
    return {"leaves": leaves, "coarse_local": coarse_local, "m2m": m2m, "m2l": m2l, "c2e": c2e, "l2l": l2l, "send_box": send_box, "pair_box": pair_box, "pair_partner": pair_partner, "pair_op": pair_op}


def translate(table_rows, sources, operator_ids, targets, in_use, operators, target_count):
    count = operator_ids.shape[0]
    order = jnp.argsort(operator_ids, stable=True).astype(jnp.int32)
    sorted_ids = operator_ids[order]
    starts = jnp.searchsorted(sorted_ids, jnp.arange(NOPS, dtype=jnp.int32)).astype(jnp.int32)
    ranks = jnp.arange(count, dtype=jnp.int32) - starts[sorted_ids]
    bucket = jnp.full((NOPS * OPCAP,), count, jnp.int32).at[sorted_ids * OPCAP + ranks].set(order)
    dump_source = table_rows.shape[0]
    source_ext = jnp.concatenate([jnp.where(in_use, sources, dump_source), jnp.full((1,), dump_source, jnp.int32)])
    target_ext = jnp.concatenate([jnp.where(in_use, targets, target_count), jnp.full((1,), target_count, jnp.int32)])
    padded = jnp.concatenate([table_rows, jnp.zeros((1, table_rows.shape[1]), table_rows.dtype)])
    gathered = padded[source_ext[bucket]].reshape(NOPS, OPCAP, table_rows.shape[1])
    images = jnp.einsum("kcj,kji->kci", gathered.astype(jnp.float32), operators, precision=lax.Precision.HIGHEST)
    summed = jax.ops.segment_sum(images.reshape(NOPS * OPCAP, table_rows.shape[1]), target_ext[bucket], num_segments=target_count + 1)
    return summed[:target_count]


def reference(leaves, coarse_local, m2m, m2l, c2e, l2l, send_box, pair_box, pair_partner, pair_op):
    devices = N_SLAB * N_SUB
    ordered = jnp.roll(leaves, -LEAD, axis=0).astype(jnp.float32).reshape(PARENTS, 8, DENS)
    upward = jnp.einsum("poj,oji->pi", ordered, m2m.astype(jnp.float32), precision=lax.Precision.HIGHEST)
    upward = upward.astype(jnp.bfloat16)
    padded_up = jnp.concatenate([upward, jnp.zeros((1, DENS), jnp.bfloat16)])
    slot_boxes = send_box.reshape(devices, devices, CAP)
    owner_base = (jnp.arange(devices, dtype=jnp.int32) * PB)[:, None, None]
    global_rows = jnp.where(slot_boxes >= 0, owner_base + slot_boxes, devices * PB).astype(jnp.int32)
    by_receiver = jnp.transpose(global_rows, (1, 0, 2)).reshape(devices, devices * CAP)
    operators = m2l.astype(jnp.float32)

    def one_device(inputs):
        rank, incoming_rows, own_boxes, partners, operator_ids = inputs
        own = lax.dynamic_slice_in_dim(upward, rank * PB, PB, 0)
        table_rows = jnp.concatenate([own, padded_up[incoming_rows]])
        in_use = partners >= 0
        safe_partner = jnp.where(in_use, partners, 0).astype(jnp.int32)
        forward = translate(table_rows, safe_partner, operator_ids, own_boxes, in_use, operators, PB)
        backward = translate(table_rows, own_boxes, (NOPS - 1 - operator_ids).astype(jnp.int32), safe_partner, in_use, operators, PB + devices * CAP)
        return forward + backward[:PB], backward[PB:]

    local_sums, remote_sums = lax.map(one_device, (jnp.arange(devices, dtype=jnp.int32), by_receiver, pair_box.reshape(devices, PAIRS), pair_partner.reshape(devices, PAIRS), pair_op.reshape(devices, PAIRS)))
    returned = jax.ops.segment_sum(remote_sums.reshape(devices * devices * CAP, DENS), by_receiver.reshape(-1), num_segments=devices * PB + 1)
    check = local_sums.reshape(devices * PB, DENS) + returned[:devices * PB]
    parent_local = (jnp.dot(check, c2e, precision=lax.Precision.HIGHEST, preferred_element_type=jnp.float32) + coarse_local.astype(jnp.float32)).astype(jnp.bfloat16)
    descended = jnp.einsum("pj,oji->poi", parent_local.astype(jnp.float32), l2l.astype(jnp.float32), precision=lax.Precision.HIGHEST)
    return parent_local, jnp.roll(descended.reshape(LEAVES, DENS), LEAD, axis=0)
```

```python
import functools

import jax
import jax.numpy as jnp
import numpy as np
from jax import lax
from jax.experimental import pallas as pl
from jax.experimental.pallas import tpu as pltpu
from jax.sharding import PartitionSpec as P
f32=jnp.float32; bf16=jnp.bfloat16
NOPS=316; CAP=20; LEAD=300; OPCAP=13
RUNS=320; SLOTS=4160; COLS=4224; GROUP=8
def pack_maps():
    row=np.arange(192)[:,None]; col=np.arange(160)[None,:]
    same=row//24==col//20
    main=same&(row%24==col%20)
    tail=same&(row%24==20+col%20//5)
    lane=np.arange(128)
    mask=(lane[None,:]//24==np.arange(160)[:,None]%5)
    fold=(lane[:,None]%24==lane[None,:])&(lane[:,None]<120)&(lane[None,:]<24)
    return main,tail,mask,fold
def translate_runs(ids,src,table,t_ref,xs,ymain,ytail):
    def group(g,_):
        for u in range(GROUP):
            r=g*GROUP+u
            k=ids[r]
            for c in range(OPCAP):
                i=pl.multiple_of(src[r*OPCAP+c],2)
                xs[u,2*c:2*c+2,:]=table[pl.ds(i,2),:]
            main=xs[u,pl.ds(0,16,stride=2),:]
            tail=xs[u,pl.ds(1,16,stride=2),:]
            x=jnp.concatenate([main,tail[:,:24]],axis=1).astype(bf16)
            y=jnp.dot(x,t_ref[k],preferred_element_type=f32)
            base=g*(GROUP*OPCAP)+u*OPCAP
            ymain[pl.ds(base,16),:]=y[:,:128]
            ytail[pl.ds(base,16),0:24]=y[:,128:]
        return 0
    lax.fori_loop(0,RUNS//GROUP,group,0)
def store_rows(table,first,main,tail):
    n=main.shape[0]
    table[pl.ds(first,n,stride=2),:]=main
    table[pl.ds(first+1,n,stride=2),:]=tail
def widen(rows):
    up=rows.astype(f32)
    return up[:,:128],jnp.concatenate([up[:,128:],jnp.zeros((up.shape[0],104),f32)],axis=1)
def backward_kernel(ids,src,up_ref,partner_ref,pm_ref,pt_ref,mask_ref,rep_ref,t_ref,local_ref,out_ref,t_out,table,xs,ymain,ytail,yb):
    xs[...]=jnp.zeros_like(xs)
    ymain[4096:,:]=jnp.zeros((ymain.shape[0]-4096,128),f32)
    ytail[...]=jnp.zeros_like(ytail)
    m,t=widen(up_ref[...])
    store_rows(table,0,m,t)
    translate_runs(ids,src,table,t_ref,xs,ymain,ytail)
    def conv(i,_):
        s=pl.ds(pl.multiple_of(i*128,128),128)
        yb[s,0:128]=ymain[s,:].astype(bf16)
        yb[s,128:256]=ytail[s,:].astype(bf16)
        return 0
    lax.fori_loop(0,COLS//128,conv,0,unroll=3)
    partner=partner_ref[...]
    def sums(first,n):
        rows=lax.broadcasted_iota(jnp.int32,(n,COLS),0)+first
        hot=jnp.where(rows==partner,1.0,0.0).astype(bf16)
        return jnp.dot(hot,yb[...],preferred_element_type=f32)
    own=sums(0,64)
    local_ref[...]=own[:,:152]
    def step(g,_):
        a=sums(64+320*g,320)
        for h in range(2):
            part=a[160*h:160*h+160]
            main=part[:,:128].astype(bf16)
            tail=(jnp.dot(part[:,128:].astype(bf16),rep_ref[...],preferred_element_type=f32)*mask_ref[...]).astype(bf16)
            packed=jnp.dot(pm_ref[...],main,preferred_element_type=f32)+jnp.dot(pt_ref[...],tail,preferred_element_type=f32)
            out_ref[pl.ds(pl.multiple_of(384*g+192*h,192),192),:]=packed.astype(bf16)
        return 0
    lax.fori_loop(0,8,step,0)
def forward_kernel(ids,src,up_ref,came_ref,box_ref,pm_ref,pt_ref,mask_ref,fold_ref,t_ref,own_ref,table,xs,ymain,ytail,yb):
    xs[...]=jnp.zeros_like(xs)
    ymain[4096:,:]=jnp.zeros((ymain.shape[0]-4096,128),f32)
    ytail[...]=jnp.zeros_like(ytail)
    m,t=widen(up_ref[...])
    store_rows(table,0,m,t)
    table[5248:5264,:]=jnp.zeros((16,128),f32)
    def unpack(g,_):
        rows=came_ref[pl.ds(pl.multiple_of(192*g,192),192),:]
        main=jnp.dot(pm_ref[...],rows,preferred_element_type=f32)
        tail=(jnp.dot(pt_ref[...],rows,preferred_element_type=f32)*mask_ref[...]).astype(bf16)
        tail=jnp.dot(tail,fold_ref[...],preferred_element_type=f32)
        store_rows(table,128+320*g,main,tail)
        return 0
    lax.fori_loop(0,16,unpack,0,unroll=2)
    translate_runs(ids,src,table,t_ref,xs,ymain,ytail)
    def conv(i,_):
        s=pl.ds(pl.multiple_of(i*128,128),128)
        yb[s,0:128]=ymain[s,:].astype(bf16)
        yb[s,128:256]=ytail[s,:].astype(bf16)
        return 0
    lax.fori_loop(0,COLS//128,conv,0,unroll=3)
    rows=lax.broadcasted_iota(jnp.int32,(64,COLS),0)
    hot=jnp.where(rows==box_ref[...],1.0,0.0).astype(bf16)
    own_ref[...]=jnp.dot(hot,yb[...],preferred_element_type=f32)[:,:152]
SM=pl.BlockSpec(memory_space=pltpu.SMEM); VM=pl.BlockSpec(memory_space=pltpu.VMEM)
def scratch(rows):
    return [pltpu.VMEM((rows,128),f32),pltpu.VMEM((GROUP,32,128),f32),pltpu.VMEM((COLS,128),f32),pltpu.VMEM((COLS,128),f32),pltpu.VMEM((COLS,256),bf16)]
LIM=16*1024*1024
def backward(ids,src,up,partner_row,t):
    main,tail,mask,fold=pack_maps()
    c=lambda a,d: jnp.asarray(a.astype(np.float32),d)
    return pl.pallas_call(backward_kernel,in_specs=[SM,SM]+[VM]*7,out_specs=[VM,VM,VM],input_output_aliases={8:2},
        out_shape=[jax.ShapeDtypeStruct((64,152),f32),jax.ShapeDtypeStruct((3072,128),bf16),pltpu.VMEM((NOPS,152,152),bf16)],
        scratch_shapes=scratch(128),compiler_params=pltpu.CompilerParams(vmem_limit_bytes=LIM),name="backward")(
        ids,src,up,partner_row,c(main,bf16),c(tail,bf16),c(mask,f32),c(fold.T,bf16),t)
def forward(ids,src,up,came,box_row,t):
    main,tail,mask,fold=pack_maps()
    c=lambda a,d: jnp.asarray(a.astype(np.float32),d)
    return pl.pallas_call(forward_kernel,in_specs=[SM,SM]+[VM]*8,out_specs=VM,
        out_shape=jax.ShapeDtypeStruct((64,152),f32),
        scratch_shapes=scratch(5264),compiler_params=pltpu.CompilerParams(vmem_limit_bytes=LIM),name="forward")(
        ids,src,up,came,box_row,c(main.T,bf16),c(tail.T,bf16),c(mask,f32),c(fold,bf16),t)
HALF=76
def operator_kernel(m_ref,o_ref,s1,s2):
    stride=153; first=pl.program_id(0)*128; j0=pl.program_id(1)*HALF
    def turn(j,_):
        t=m_ref[j].T.astype(f32)
        s1[pl.ds(j0+j,128,stride=stride),:]=t[:,:128]
        s2[pl.ds(j0+j,128,stride=stride),0:24]=t[:,128:]
        return 0
    lax.fori_loop(0,HALF,turn,0,unroll=4)
    @pl.when(pl.program_id(1)==1)
    def _():
        def collect(k,_):
            o_ref[first+k,:,0:128]=s1[pl.ds(k*stride,152),:].astype(bf16)
            o_ref[first+k,:,128:152]=s2[pl.ds(k*stride,152),:][:,:24].astype(bf16)
            return 0
        lax.fori_loop(0,jnp.minimum(128,NOPS-first),collect,0)
def operators(m):
    t=pl.pallas_call(operator_kernel,grid=(3,2),in_specs=[pl.BlockSpec((HALF,152,128),lambda i,j:(j,0,i))],
      out_specs=VM,out_shape=pltpu.VMEM((NOPS,152,152),bf16),
      scratch_shapes=[pltpu.VMEM((128*153,128),f32)]*2,
      compiler_params=pltpu.CompilerParams(vmem_limit_bytes=27*1024*1024),name="operators")(m)
    return t

def slot_rows(send):
    flat=jnp.pad(send,((0,0),(0,4)),constant_values=-1).reshape(1,3072)
    parts=[flat]
    split=send.reshape(128,4,5)
    for t in range(5):
        parts.append(jnp.pad(split[:,:,t],((0,0),(20,0)),constant_values=-1).reshape(1,3072))
    return jnp.concatenate(parts+[jnp.full((2,3072),-1,jnp.int32)])
def slot_hot(slot_ref):
    boxes=lax.broadcasted_iota(jnp.int32,(64,3072),0)
    return [jnp.where(boxes==slot_ref[b:b+1,:],1.0,0.0).astype(bf16) for b in range(6)]
def send_kernel(slot_ref,up_ref,rep_ref,out_ref):
    up=up_ref[...]
    tail=jnp.dot(jnp.concatenate([up[:,128:],jnp.zeros((64,104),bf16)],axis=1),rep_ref[...],preferred_element_type=f32)
    lane=lax.broadcasted_iota(jnp.int32,(64,128),1)
    values=[up[:,:128]]+[jnp.where((lane>=24*t)&(lane<24*t+24),tail,0.0).astype(bf16) for t in range(5)]
    hot=jnp.concatenate(slot_hot(slot_ref),axis=0)
    out_ref[...]=lax.dot_general(hot,jnp.concatenate(values,axis=0),(((0,),(0,)),((),())),preferred_element_type=f32).astype(bf16)
def pack_sends(slots,up):
    fold=pack_maps()[3]
    return pl.pallas_call(send_kernel,in_specs=[VM]*3,out_specs=VM,out_shape=jax.ShapeDtypeStruct((3072,128),bf16),
        compiler_params=pltpu.CompilerParams(vmem_limit_bytes=LIM),name="send")(slots,up,jnp.asarray(fold.T.astype(np.float32),bf16))
def finish_kernel(slot_ref,came_ref,local_ref,own_ref,c2e_ref,coarse_ref,parent_ref):
    hot=jnp.concatenate(slot_hot(slot_ref),axis=0)
    got=jnp.dot(hot,came_ref[...],preferred_element_type=f32)
    tail=got[64:128,0:24]
    for t in range(1,5):
        tail=tail+got[64+64*t:128+64*t,24*t:24*t+24]
    check=local_ref[...]+own_ref[...]+jnp.concatenate([got[:64],tail],axis=1)
    parent=jnp.dot(check,c2e_ref[...],precision=lax.Precision.HIGHEST,preferred_element_type=f32)+coarse_ref[...].astype(f32)
    parent_ref[...]=parent.astype(bf16)
def finish(slots,came,local,own,c2e,coarse):
    return pl.pallas_call(finish_kernel,in_specs=[VM]*6,out_specs=VM,out_shape=jax.ShapeDtypeStruct((64,152),bf16),
        compiler_params=pltpu.CompilerParams(vmem_limit_bytes=LIM),name="finish")(slots,came,local,own,c2e,coarse)
def pad_to(a,n,v):
    return jnp.concatenate([a,jnp.full((n-a.shape[0],),v,a.dtype)])
AXES=("slab","sub")
def shifted(x, by):
    count = lax.axis_size(AXES)
    return lax.ppermute(x, AXES, [(i, (i + by) % count) for i in range(count)])
def exchange(x):
    return lax.all_to_all(x.reshape(128,24,128),AXES,split_axis=0,concat_axis=0,tiled=True).reshape(3072,128)
def shards(leaves, coarse_local, m2m, m2l, c2e, l2l, send_box, pair_box, pair_partner, pair_op):
    width=152; box_count=64; edge=38
    front=jnp.concatenate([jnp.zeros((8*edge-LEAD,width),bf16),leaves[:LEAD]])
    front_sum=jnp.einsum("poj,oji->pi",front.reshape(edge,8,width),m2m,preferred_element_type=f32)
    arrived=shifted(front_sum,-1)
    ops=operators(jnp.transpose(m2l,(1,2,0)))
    own_rows=jnp.concatenate([leaves[LEAD:],jnp.zeros((LEAD,width),bf16)])
    up_sum=jnp.einsum("poj,oji->pi",own_rows.reshape(box_count,8,width),m2m,preferred_element_type=f32)
    up=up_sum.at[box_count-edge:].add(arrived).astype(bf16)
    slots=slot_rows(send_box.reshape(128,CAP))
    ids=pair_op.reshape(NOPS,OPCAP)[:,0]
    ids_f=pad_to(ids,RUNS,0); ids_b=pad_to(NOPS-1-ids,RUNS,0)
    src_f=pad_to(2*jnp.where(pair_partner>=0,pair_partner,2624),SLOTS,2*2624)
    src_b=pad_to(2*pair_box,SLOTS,0)
    partner_row=pad_to(pair_partner,COLS,-1)[None]
    box_row=pad_to(pair_box,COLS,-1)[None]
    came=exchange(pack_sends(slots,up))
    ops=pltpu.with_memory_space_constraint(ops,pltpu.VMEM)
    local,to_owners,ops=backward(ids_b,src_b,up,partner_row,ops)
    returned=exchange(to_owners)
    ops=pltpu.with_memory_space_constraint(ops,pltpu.VMEM)
    own=forward(ids_f,src_f,up,came,box_row,ops)
    parent=finish(slots,returned,local,own,c2e,coarse_local)
    earlier=shifted(parent[box_count-edge:],1)
    head=jnp.einsum("pj,oji->poi",earlier,l2l,preferred_element_type=f32).reshape(8*edge,width)
    own_part=jnp.einsum("pj,oji->poi",parent,l2l,preferred_element_type=f32).reshape(8*box_count,width)
    leaf_local=jnp.concatenate([head[8*edge-LEAD:],own_part[:8*box_count-LEAD]])
    return (parent,leaf_local)


def solution(mesh):
    split = P(("slab", "sub"), None)
    flat = P(("slab", "sub"))
    return jax.shard_map(
        shards,
        mesh=mesh,
        in_specs=(split, split, P(), P(), P(), P(), split, flat, flat, flat),
        out_specs=(split, split),
        check_vma=False,
    )
```

```python
import functools

import jax
import jax.numpy as jnp
import numpy as np
from jax import lax
from jax.experimental import pallas as pl
from jax.experimental.pallas import tpu as pltpu
from jax.sharding import PartitionSpec as P
f32=jnp.float32; bf16=jnp.bfloat16
NOPS=316; CAP=20; LEAD=300; OPCAP=13
RUNS=320; SLOTS=4160; COLS=4224; GROUP=32
def pack_maps():
    row=np.arange(192)[:,None]; col=np.arange(160)[None,:]
    same=row//24==col//20
    main=same&(row%24==col%20)
    tail=same&(row%24==20+col%20//5)
    lane=np.arange(128)
    mask=(lane[None,:]//24==np.arange(160)[:,None]%5)
    fold=(lane[:,None]%24==lane[None,:])&(lane[:,None]<120)&(lane[None,:]<24)
    return main,tail,mask,fold
NACC=4
CHUNK=64
def fetch_operators(t_ref,t_buf,sems):
    copies=[]
    for q in range(5):
        n=min(CHUNK,NOPS-q*CHUNK)
        copies.append(pltpu.make_async_copy(t_ref.at[pl.ds(q*CHUNK,n)],t_buf.at[pl.ds(q*CHUNK,n)],sems.at[q]))
        copies[-1].start()
    return copies
def translate_runs(places,src,dst,flip,copies,table,t_buf,xs,ys,accs):
    def group(g,_):
        for u in range(GROUP):
            k=g*GROUP+u
            first=places[NOPS-1-k if flip else k] if u<GROUP-4 else places[jnp.where(k<NOPS,NOPS-1-k,k) if flip else k]
            for c in range(OPCAP):
                i=pl.multiple_of(src[first+c],2)
                xs[u,2*c:2*c+2,:]=table[pl.ds(i,2),:]
            main=xs[u,pl.ds(0,16,stride=2),:]
            tail=xs[u,pl.ds(1,16,stride=2),:]
            x=jnp.concatenate([main,tail[:,:24]],axis=1).astype(bf16)
            y=jnp.dot(x,t_buf[jnp.minimum(k,NOPS-1)],preferred_element_type=f32)
            ys[u,pl.ds(0,16,stride=2),:]=y[:,:128]
            ys[u,pl.ds(1,16,stride=2),0:24]=y[:,128:]
            for c in range(OPCAP):
                d=pl.multiple_of(dst[first+c],2)
                acc=accs[(u*OPCAP+c)%NACC]
                acc[pl.ds(d,2),:]=acc[pl.ds(d,2),:]+ys[u,2*c:2*c+2,:]
        return 0
    for q in range(5):
        copies[q].wait()
        lax.fori_loop(q*CHUNK//GROUP,(q+1)*CHUNK//GROUP,group,0)
def zero_fill(ref):
    n=ref.shape[0]
    def fill(i,_):
        ref[pl.ds(pl.multiple_of(i*64,64),64),:]=jnp.zeros((64,128),f32)
        return 0
    lax.fori_loop(0,n//64,fill,0,unroll=4)
def sum_rows(accs,first,n):
    main=accs[0][pl.ds(first,n,stride=2),:]
    tail=accs[0][pl.ds(first+1,n,stride=2),:]
    for acc in accs[1:]:
        main=main+acc[pl.ds(first,n,stride=2),:]
        tail=tail+acc[pl.ds(first+1,n,stride=2),:]
    lane=lax.broadcasted_iota(jnp.int32,tail.shape,1)
    return main,jnp.where(lane<24,tail,0.0)
def store_rows(table,first,main,tail):
    n=main.shape[0]
    table[pl.ds(first,n,stride=2),:]=main
    table[pl.ds(first+1,n,stride=2),:]=tail
def widen(rows):
    up=rows.astype(f32)
    return up[:,:128],jnp.concatenate([up[:,128:],jnp.zeros((up.shape[0],104),f32)],axis=1)
def backward_kernel(places,src,dst,up_ref,pm_ref,pt_ref,mask_ref,rep_ref,t_ref,local_ref,out_ref,t_buf,sems,table,xs,ys,*accs):
    copies=fetch_operators(t_ref,t_buf,sems)
    xs[...]=jnp.zeros_like(xs)
    ys[...]=jnp.zeros_like(ys)
    for acc in accs:
        zero_fill(acc)
    m,t=widen(up_ref[...])
    store_rows(table,0,m,t)
    translate_runs(places,src,dst,True,copies,table,t_buf,xs,ys,accs)
    m,t=sum_rows(accs,0,64)
    local_ref[:,:128]=m
    local_ref[:,128:]=t[:,:24]
    def step(g,_):
        main,tail=sum_rows(accs,128+320*g,160)
        tail=(jnp.dot(tail.astype(bf16),rep_ref[...],preferred_element_type=f32)*mask_ref[...]).astype(bf16)
        packed=jnp.dot(pm_ref[...],main.astype(bf16),preferred_element_type=f32)+jnp.dot(pt_ref[...],tail,preferred_element_type=f32)
        out_ref[pl.ds(pl.multiple_of(192*g,192),192),:]=packed.astype(bf16)
        return 0
    lax.fori_loop(0,16,step,0,unroll=2)
def forward_kernel(places,src,dst,up_ref,came_ref,pm_ref,pt_ref,mask_ref,fold_ref,t_ref,own_ref,t_buf,sems,table,xs,ys,*accs):
    copies=fetch_operators(t_ref,t_buf,sems)
    xs[...]=jnp.zeros_like(xs)
    ys[...]=jnp.zeros_like(ys)
    for acc in accs:
        acc[...]=jnp.zeros_like(acc)
    m,t=widen(up_ref[...])
    store_rows(table,0,m,t)
    table[5248:5264,:]=jnp.zeros((16,128),f32)
    def unpack(g,_):
        rows=came_ref[pl.ds(pl.multiple_of(192*g,192),192),:]
        main=jnp.dot(pm_ref[...],rows,preferred_element_type=f32)
        tail=(jnp.dot(pt_ref[...],rows,preferred_element_type=f32)*mask_ref[...]).astype(bf16)
        tail=jnp.dot(tail,fold_ref[...],preferred_element_type=f32)
        store_rows(table,128+320*g,main,tail)
        return 0
    lax.fori_loop(0,16,unpack,0,unroll=4)
    translate_runs(places,src,dst,False,copies,table,t_buf,xs,ys,accs)
    m,t=sum_rows(accs,0,64)
    own_ref[:,:128]=m
    own_ref[:,128:]=t[:,:24]
SM=pl.BlockSpec(memory_space=pltpu.SMEM); VM=pl.BlockSpec(memory_space=pltpu.VMEM)
def scratch(rows,acc_rows):
    return [pltpu.VMEM((NOPS,152,152),bf16),pltpu.SemaphoreType.DMA((5,)),pltpu.VMEM((rows,128),f32),pltpu.VMEM((GROUP,32,128),f32),pltpu.VMEM((GROUP,32,128),f32)]+[pltpu.VMEM((acc_rows,128),f32)]*NACC
LIM=46*1024*1024
ANY=pl.BlockSpec(memory_space=pl.ANY)
def backward(places,src,dst,up,t):
    main,tail,mask,fold=pack_maps()
    c=lambda a,d: jnp.asarray(a.astype(np.float32),d)
    return pl.pallas_call(backward_kernel,in_specs=[SM]*3+[VM]*5+[ANY],out_specs=[VM,VM],
        out_shape=[jax.ShapeDtypeStruct((64,152),f32),jax.ShapeDtypeStruct((3072,128),bf16)],
        scratch_shapes=scratch(128,5312),compiler_params=pltpu.CompilerParams(vmem_limit_bytes=LIM),name="backward")(
        places,src,dst,up,c(main,bf16),c(tail,bf16),c(mask,f32),c(fold.T,bf16),t)
def forward(places,src,dst,up,came,t):
    main,tail,mask,fold=pack_maps()
    c=lambda a,d: jnp.asarray(a.astype(np.float32),d)
    return pl.pallas_call(forward_kernel,in_specs=[SM]*3+[VM]*6+[ANY],out_specs=VM,
        out_shape=jax.ShapeDtypeStruct((64,152),f32),
        scratch_shapes=scratch(5264,128),compiler_params=pltpu.CompilerParams(vmem_limit_bytes=LIM),name="forward")(
        places,src,dst,up,came,c(main.T,bf16),c(tail.T,bf16),c(mask,f32),c(fold,bf16),t)
def operator_kernel(m_ref,t_ref,s1,s2):
    part=pl.program_id(1)
    def turn(j,_):
        t=m_ref[j].T.astype(f32)
        s1[pl.ds(part*76+j,128,stride=153),:]=t[:,:128]
        s2[pl.ds(part*76+j,128,stride=153),0:24]=t[:,128:]
        return 0
    lax.fori_loop(0,76,turn,0,unroll=UN)
    @pl.when(part==1)
    def _():
        def collect(k,_):
            t_ref[k,:,0:128]=s1[pl.ds(k*153,152),:].astype(bf16)
            t_ref[k,:,128:152]=s2[pl.ds(k*153,152),:][:,:24].astype(bf16)
            return 0
        lax.fori_loop(0,128,collect,0,unroll=4)
UN=19
def operators(m):
    return pl.pallas_call(operator_kernel,grid=(3,2),in_specs=[pl.BlockSpec((76,152,128),lambda i,j:(j,0,i))],
      out_specs=pl.BlockSpec((128,152,152),lambda i,j:(i,0,0)),out_shape=jax.ShapeDtypeStruct((NOPS,152,152),bf16),
      scratch_shapes=[pltpu.VMEM((128*153,128),f32)]*2,
      compiler_params=pltpu.CompilerParams(vmem_limit_bytes=50*1024*1024),name="operators")(m)

def slot_rows(send):
    flat=jnp.pad(send,((0,0),(0,4)),constant_values=-1).reshape(1,3072)
    parts=[flat]
    split=send.reshape(128,4,5)
    for t in range(5):
        parts.append(jnp.pad(split[:,:,t],((0,0),(20,0)),constant_values=-1).reshape(1,3072))
    return jnp.concatenate(parts+[jnp.full((2,3072),-1,jnp.int32)])
def slot_hot(slot_ref):
    boxes=lax.broadcasted_iota(jnp.int32,(64,3072),0)
    return [jnp.where(boxes==slot_ref[b:b+1,:],1.0,0.0).astype(bf16) for b in range(6)]
def send_kernel(slot_ref,up_ref,rep_ref,out_ref):
    up=up_ref[...]
    tail=jnp.dot(jnp.concatenate([up[:,128:],jnp.zeros((64,104),bf16)],axis=1),rep_ref[...],preferred_element_type=f32)
    lane=lax.broadcasted_iota(jnp.int32,(64,128),1)
    values=[up[:,:128]]+[jnp.where((lane>=24*t)&(lane<24*t+24),tail,0.0).astype(bf16) for t in range(5)]
    hot=jnp.concatenate(slot_hot(slot_ref),axis=0)
    out_ref[...]=lax.dot_general(hot,jnp.concatenate(values,axis=0),(((0,),(0,)),((),())),preferred_element_type=f32).astype(bf16)
def pack_sends(slots,up):
    fold=pack_maps()[3]
    return pl.pallas_call(send_kernel,in_specs=[VM]*3,out_specs=VM,out_shape=jax.ShapeDtypeStruct((3072,128),bf16),
        compiler_params=pltpu.CompilerParams(vmem_limit_bytes=LIM),name="send")(slots,up,jnp.asarray(fold.T.astype(np.float32),bf16))
def finish_kernel(slot_ref,came_ref,local_ref,own_ref,c2e_ref,coarse_ref,parent_ref):
    hot=jnp.concatenate(slot_hot(slot_ref),axis=0)
    got=jnp.dot(hot,came_ref[...],preferred_element_type=f32)
    tail=got[64:128,0:24]
    for t in range(1,5):
        tail=tail+got[64+64*t:128+64*t,24*t:24*t+24]
    check=local_ref[...]+own_ref[...]+jnp.concatenate([got[:64],tail],axis=1)
    parent=jnp.dot(check,c2e_ref[...],precision=lax.Precision.HIGHEST,preferred_element_type=f32)+coarse_ref[...].astype(f32)
    parent_ref[...]=parent.astype(bf16)
def finish(slots,came,local,own,c2e,coarse):
    return pl.pallas_call(finish_kernel,in_specs=[VM]*6,out_specs=VM,out_shape=jax.ShapeDtypeStruct((64,152),bf16),
        compiler_params=pltpu.CompilerParams(vmem_limit_bytes=LIM),name="finish")(slots,came,local,own,c2e,coarse)
def pad_to(a,n,v):
    return jnp.concatenate([a,jnp.full((n-a.shape[0],),v,a.dtype)])
AXES=("slab","sub")
def shifted(x, by):
    count = lax.axis_size(AXES)
    return lax.ppermute(x, AXES, [(i, (i + by) % count) for i in range(count)])
def run_places(ids):
    run=jnp.arange(RUNS,dtype=jnp.int32)
    first=jnp.sum(jnp.where(pad_to(ids,RUNS,-1)[None,:]==run[:,None],OPCAP*run[None,:],0),axis=1)
    return jnp.where(run<NOPS,first,OPCAP*run)
def exchange(x):
    return lax.all_to_all(x.reshape(128,24,128),AXES,split_axis=0,concat_axis=0,tiled=True).reshape(3072,128)
def shards(leaves, coarse_local, m2m, m2l, c2e, l2l, send_box, pair_box, pair_partner, pair_op):
    width=152; box_count=64; edge=38
    front=jnp.concatenate([jnp.zeros((8*edge-LEAD,width),bf16),leaves[:LEAD]])
    front_sum=jnp.einsum("poj,oji->pi",front.reshape(edge,8,width),m2m,preferred_element_type=f32)
    arrived=shifted(front_sum,-1)
    ops=operators(jnp.transpose(m2l,(1,2,0)))
    own_rows=jnp.concatenate([leaves[LEAD:],jnp.zeros((LEAD,width),bf16)])
    up_sum=jnp.einsum("poj,oji->pi",own_rows.reshape(box_count,8,width),m2m,preferred_element_type=f32)
    up=up_sum.at[box_count-edge:].add(arrived).astype(bf16)
    slots=slot_rows(send_box.reshape(128,CAP))
    places=run_places(pair_op.reshape(NOPS,OPCAP)[:,0])
    partner=pad_to(2*jnp.where(pair_partner>=0,pair_partner,2624),SLOTS,2*2624)
    box=pad_to(2*pair_box,SLOTS,0)
    came=exchange(pack_sends(slots,up))
    local,to_owners=backward(places,box,partner,up,ops)
    returned=exchange(to_owners)
    own=forward(places,partner,box,up,came,ops)
    parent=finish(slots,returned,local,own,c2e,coarse_local)
    earlier=shifted(parent[box_count-edge:],1)
    head=jnp.einsum("pj,oji->poi",earlier,l2l,preferred_element_type=f32).reshape(8*edge,width)
    own_part=jnp.einsum("pj,oji->poi",parent,l2l,preferred_element_type=f32).reshape(8*box_count,width)
    leaf_local=jnp.concatenate([head[8*edge-LEAD:],own_part[:8*box_count-LEAD]])
    return (parent,leaf_local)


def solution(mesh):
    split = P(("slab", "sub"), None)
    flat = P(("slab", "sub"))
    return jax.shard_map(
        shards,
        mesh=mesh,
        in_specs=(split, split, P(), P(), P(), P(), split, flat, flat, flat),
        out_specs=(split, split),
        check_vma=False,
    )
```

```python
import functools

import jax
import jax.numpy as jnp
import numpy as np
from jax import lax
from jax.experimental import pallas as pl
from jax.experimental.pallas import tpu as pltpu
from jax.sharding import PartitionSpec as P
f32=jnp.float32; bf16=jnp.bfloat16
NOPS=316; CAP=20; LEAD=300; OPCAP=13
RUNS=320; SLOTS=4160; COLS=4224; GROUP=32
def pack_maps():
    row=np.arange(192)[:,None]; col=np.arange(160)[None,:]
    same=row//24==col//20
    main=same&(row%24==col%20)
    tail=same&(row%24==20+col%20//5)
    lane=np.arange(128)
    mask=(lane[None,:]//24==np.arange(160)[:,None]%5)
    fold=(lane[:,None]%24==lane[None,:])&(lane[:,None]<120)&(lane[None,:]<24)
    return main,tail,mask,fold
NACC=4
CHUNK=64
def fetch_operators(t_ref,t_buf,sems):
    copies=[]
    for q in range(5):
        n=min(CHUNK,NOPS-q*CHUNK)
        copies.append(pltpu.make_async_copy(t_ref.at[pl.ds(q*CHUNK,n)],t_buf.at[pl.ds(q*CHUNK,n)],sems.at[q]))
        copies[-1].start()
    return copies
def translate_runs(places,src,dst,flip,copies,table,t_buf,xs,ys,accs):
    def group(g,_):
        for u in range(GROUP):
            k=g*GROUP+u
            first=places[NOPS-1-k if flip else k] if u<GROUP-4 else places[jnp.where(k<NOPS,NOPS-1-k,k) if flip else k]
            for c in range(OPCAP):
                i=pl.multiple_of(src[first+c],2)
                xs[u,2*c:2*c+2,:]=table[pl.ds(i,2),:]
            main=xs[u,pl.ds(0,16,stride=2),:]
            tail=xs[u,pl.ds(1,16,stride=2),:]
            x=jnp.concatenate([main,tail[:,:24]],axis=1).astype(bf16)
            y=jnp.dot(x,t_buf[jnp.minimum(k,NOPS-1)],preferred_element_type=f32)
            ys[u,pl.ds(0,16,stride=2),:]=y[:,:128]
            ys[u,pl.ds(1,16,stride=2),0:24]=y[:,128:]
            for c in range(OPCAP):
                d=pl.multiple_of(dst[first+c],2)
                acc=accs[(u*OPCAP+c)%NACC]
                acc[pl.ds(d,2),:]=acc[pl.ds(d,2),:]+ys[u,2*c:2*c+2,:]
        return 0
    for q in range(5):
        copies[q].wait()
        lax.fori_loop(q*CHUNK//GROUP,(q+1)*CHUNK//GROUP,group,0)
def zero_fill(ref):
    n=ref.shape[0]
    def fill(i,_):
        ref[pl.ds(pl.multiple_of(i*64,64),64),:]=jnp.zeros((64,128),f32)
        return 0
    lax.fori_loop(0,n//64,fill,0,unroll=4)
def sum_rows(accs,first,n):
    main=accs[0][pl.ds(first,n,stride=2),:]
    tail=accs[0][pl.ds(first+1,n,stride=2),:]
    for acc in accs[1:]:
        main=main+acc[pl.ds(first,n,stride=2),:]
        tail=tail+acc[pl.ds(first+1,n,stride=2),:]
    lane=lax.broadcasted_iota(jnp.int32,tail.shape,1)
    return main,jnp.where(lane<24,tail,0.0)
def store_rows(table,first,main,tail):
    n=main.shape[0]
    table[pl.ds(first,n,stride=2),:]=main
    table[pl.ds(first+1,n,stride=2),:]=tail
def widen(rows):
    up=rows.astype(f32)
    return up[:,:128],jnp.concatenate([up[:,128:],jnp.zeros((up.shape[0],104),f32)],axis=1)
def backward_kernel(places,src,dst,up_ref,pm_ref,pt_ref,mask_ref,rep_ref,t_ref,local_ref,out_ref,t_buf,sems,table,xs,ys,*accs):
    copies=fetch_operators(t_ref,t_buf,sems)
    xs[...]=jnp.zeros_like(xs)
    ys[...]=jnp.zeros_like(ys)
    for acc in accs:
        zero_fill(acc)
    m,t=widen(up_ref[...])
    store_rows(table,0,m,t)
    translate_runs(places,src,dst,True,copies,table,t_buf,xs,ys,accs)
    m,t=sum_rows(accs,0,64)
    local_ref[:,:128]=m
    local_ref[:,128:]=t[:,:24]
    def step(g,_):
        main,tail=sum_rows(accs,128+320*g,160)
        tail=(jnp.dot(tail.astype(bf16),rep_ref[...],preferred_element_type=f32)*mask_ref[...]).astype(bf16)
        packed=jnp.dot(pm_ref[...],main.astype(bf16),preferred_element_type=f32)+jnp.dot(pt_ref[...],tail,preferred_element_type=f32)
        out_ref[pl.ds(pl.multiple_of(192*g,192),192),:]=packed.astype(bf16)
        return 0
    lax.fori_loop(0,16,step,0,unroll=2)
def forward_kernel(places,src,dst,up_ref,came_ref,pm_ref,pt_ref,mask_ref,fold_ref,t_ref,own_ref,t_buf,sems,table,xs,ys,*accs):
    copies=fetch_operators(t_ref,t_buf,sems)
    xs[...]=jnp.zeros_like(xs)
    ys[...]=jnp.zeros_like(ys)
    for acc in accs:
        acc[...]=jnp.zeros_like(acc)
    m,t=widen(up_ref[...])
    store_rows(table,0,m,t)
    table[5248:5264,:]=jnp.zeros((16,128),f32)
    def unpack(g,_):
        rows=came_ref[pl.ds(pl.multiple_of(192*g,192),192),:]
        main=jnp.dot(pm_ref[...],rows,preferred_element_type=f32)
        tail=(jnp.dot(pt_ref[...],rows,preferred_element_type=f32)*mask_ref[...]).astype(bf16)
        tail=jnp.dot(tail,fold_ref[...],preferred_element_type=f32)
        store_rows(table,128+320*g,main,tail)
        return 0
    lax.fori_loop(0,16,unpack,0,unroll=4)
    translate_runs(places,src,dst,False,copies,table,t_buf,xs,ys,accs)
    m,t=sum_rows(accs,0,64)
    own_ref[:,:128]=m
    own_ref[:,128:]=t[:,:24]
SM=pl.BlockSpec(memory_space=pltpu.SMEM); VM=pl.BlockSpec(memory_space=pltpu.VMEM)
def scratch(rows,acc_rows):
    return [pltpu.VMEM((NOPS,152,152),bf16),pltpu.SemaphoreType.DMA((5,)),pltpu.VMEM((rows,128),f32),pltpu.VMEM((GROUP,32,128),f32),pltpu.VMEM((GROUP,32,128),f32)]+[pltpu.VMEM((acc_rows,128),f32)]*NACC
LIM=46*1024*1024
ANY=pl.BlockSpec(memory_space=pl.ANY)
def backward(places,src,dst,up,t):
    main,tail,mask,fold=pack_maps()
    c=lambda a,d: jnp.asarray(a.astype(np.float32),d)
    return pl.pallas_call(backward_kernel,in_specs=[SM]*3+[VM]*5+[ANY],out_specs=[VM,VM],
        out_shape=[jax.ShapeDtypeStruct((64,152),f32),jax.ShapeDtypeStruct((3072,128),bf16)],
        scratch_shapes=scratch(128,5312),compiler_params=pltpu.CompilerParams(vmem_limit_bytes=LIM),name="backward")(
        places,src,dst,up,c(main,bf16),c(tail,bf16),c(mask,f32),c(fold.T,bf16),t)
def forward(places,src,dst,up,came,t):
    main,tail,mask,fold=pack_maps()
    c=lambda a,d: jnp.asarray(a.astype(np.float32),d)
    return pl.pallas_call(forward_kernel,in_specs=[SM]*3+[VM]*6+[ANY],out_specs=VM,
        out_shape=jax.ShapeDtypeStruct((64,152),f32),
        scratch_shapes=scratch(5264,128),compiler_params=pltpu.CompilerParams(vmem_limit_bytes=LIM),name="forward")(
        places,src,dst,up,came,c(main.T,bf16),c(tail.T,bf16),c(mask,f32),c(fold,bf16),t)
def operator_kernel(m_ref,t_ref,s1,s2):
    block=pl.program_id(0); part=pl.program_id(1)
    def turn(n):
        eye=(lax.broadcasted_iota(jnp.int32,(n,n),0)==lax.broadcasted_iota(jnp.int32,(n,n),1)).astype(bf16)
        def body(g,_):
            for u in range(19):
                j=19*g+u
                if u%3==2:
                    t=lax.dot_general(eye,m_ref[j,:,0:n],(((1,),(1,)),((),())),preferred_element_type=f32)
                else:
                    t=m_ref[j,:,0:n].T.astype(f32)
                s1[pl.ds(part*76+j,n,stride=153),:]=t[:,:128]
                s2[pl.ds(part*76+j,n,stride=153),0:24]=t[:,128:]
            return 0
        lax.fori_loop(0,4,body,0)
    def collect(n):
        def body(q,_):
            for u in range(4):
                k=4*q+u
                t_ref[k,:,0:128]=s1[pl.ds(k*153,152),:].astype(bf16)
                t_ref[k,:,128:152]=s2[pl.ds(k*153,152),:][:,:24].astype(bf16)
            return 0
        lax.fori_loop(0,n//4,body,0)
    @pl.when(block<2)
    def _():
        turn(128)
    @pl.when(block==2)
    def _():
        turn(64)
    @pl.when((part==1)&(block<2))
    def _():
        collect(128)
    @pl.when((part==1)&(block==2))
    def _():
        collect(60)
def operators(m):
    return pl.pallas_call(operator_kernel,grid=(3,2),in_specs=[pl.BlockSpec((76,152,128),lambda i,j:(j,0,i))],
      out_specs=pl.BlockSpec((128,152,152),lambda i,j:(i,0,0)),out_shape=jax.ShapeDtypeStruct((NOPS,152,152),bf16),
      scratch_shapes=[pltpu.VMEM((128*153,128),f32)]*2,
      compiler_params=pltpu.CompilerParams(vmem_limit_bytes=50*1024*1024),name="operators")(m)

EDGE=38
def gather_kernel(leaf_ref,m2m_ref,front_ref,own_ref):
    rows=leaf_ref[...].astype(f32).T.astype(bf16)
    box=lax.broadcasted_iota(jnp.int32,(72,512),0)
    row=lax.broadcasted_iota(jnp.int32,(72,512),1)
    total=jnp.zeros((72,152),f32)
    for c in range(8):
        hot=jnp.where(row==8*box+(c-4),1.0,0.0).astype(bf16)
        child=jnp.dot(hot,rows,preferred_element_type=f32).astype(bf16)
        total=total+jnp.dot(child,m2m_ref[c],preferred_element_type=f32)
    front_ref[...]=total[:EDGE]
    own_ref[...]=jnp.concatenate([total[EDGE:65],jnp.zeros((37,152),f32)],axis=0)
def gather_children(leaf_t,m2m):
    return pl.pallas_call(gather_kernel,in_specs=[VM]*2,out_specs=[VM]*2,
        out_shape=[jax.ShapeDtypeStruct((EDGE,152),f32),jax.ShapeDtypeStruct((64,152),f32)],
        compiler_params=pltpu.CompilerParams(vmem_limit_bytes=16*1024*1024),name="gather")(leaf_t,m2m)
def slot_hot(index_ref,g):
    boxes=lax.broadcasted_iota(jnp.int32,(64,192),0).astype(f32)+1.0
    return jnp.concatenate([jnp.where(boxes==index_ref[16*b+g:16*b+g+1,:],1.0,0.0).astype(bf16) for b in range(6)],axis=0)
def send_kernel(send_ref,own_ref,arrived_ref,pm_ref,pt_ref,rep_ref,out_ref,up_ref,index_ref):
    plus=(send_ref[...]+1).astype(f32)
    plus=jnp.concatenate([plus[:,160*g:160*g+160] for g in range(16)],axis=0)
    slot=lax.rem(lax.broadcasted_iota(jnp.int32,(16,160),1),5)
    index_ref[0:16,:]=jnp.dot(plus.astype(bf16),pm_ref[...],preferred_element_type=f32)
    for t in range(5):
        index_ref[16*t+16:16*t+32,:]=jnp.dot(jnp.where(slot==t,plus,0.0).astype(bf16),pt_ref[...],preferred_element_type=f32)
    up=(own_ref[...]+jnp.concatenate([jnp.zeros((64-EDGE,152),f32),arrived_ref[...]],axis=0)).astype(bf16)
    up_ref[...]=up
    tail=jnp.dot(jnp.concatenate([up[:,128:],jnp.zeros((64,104),bf16)],axis=1),rep_ref[...],preferred_element_type=f32)
    lane=lax.broadcasted_iota(jnp.int32,(64,128),1)
    values=jnp.concatenate([up[:,:128]]+[jnp.where((lane>=24*t)&(lane<24*t+24),tail,0.0).astype(bf16) for t in range(5)],axis=0)
    for g in range(16):
        out_ref[192*g:192*g+192,:]=lax.dot_general(slot_hot(index_ref,g),values,(((0,),(0,)),((),())),preferred_element_type=f32).astype(bf16)
def pack_sends(send,own,arrived):
    main,tail,mask,fold=pack_maps()
    c=lambda a: jnp.asarray(a.astype(np.float32),bf16)
    return pl.pallas_call(send_kernel,in_specs=[VM]*6,out_specs=[VM]*3,
        out_shape=[jax.ShapeDtypeStruct((3072,128),bf16),jax.ShapeDtypeStruct((64,152),bf16),jax.ShapeDtypeStruct((96,192),f32)],
        compiler_params=pltpu.CompilerParams(vmem_limit_bytes=16*1024*1024),name="send")(send,own,arrived,c(main.T),c(tail.T),c(fold.T))
def finish_kernel(index_ref,came_ref,local_ref,own_ref,c2e_ref,coarse_ref,parent_ref,edge_ref):
    got=jnp.zeros((384,128),f32)
    for g in range(16):
        got=got+jnp.dot(slot_hot(index_ref,g),came_ref[192*g:192*g+192,:],preferred_element_type=f32)
    tail=got[64:128,0:24]
    for t in range(1,5):
        tail=tail+got[64+64*t:128+64*t,24*t:24*t+24]
    check=local_ref[...]+own_ref[...]+jnp.concatenate([got[:64],tail],axis=1)
    parent=(jnp.dot(check,c2e_ref[...],precision=lax.Precision.HIGHEST,preferred_element_type=f32)+coarse_ref[...].astype(f32)).astype(bf16)
    parent_ref[...]=parent
    edge_ref[...]=parent[64-EDGE:]
def finish(index,came,local,own,c2e,coarse):
    return pl.pallas_call(finish_kernel,in_specs=[VM]*6,out_specs=[VM]*2,
        out_shape=[jax.ShapeDtypeStruct((64,152),bf16),jax.ShapeDtypeStruct((EDGE,152),bf16)],
        compiler_params=pltpu.CompilerParams(vmem_limit_bytes=16*1024*1024),name="finish")(index,came,local,own,c2e,coarse)
def pad_to(a,n,v):
    return jnp.concatenate([a,jnp.full((n-a.shape[0],),v,a.dtype)])
AXES=("slab","sub")
def shifted(x, by):
    count = lax.axis_size(AXES)
    return lax.ppermute(x, AXES, [(i, (i + by) % count) for i in range(count)])
def run_places(ids):
    run=jnp.arange(RUNS,dtype=jnp.int32)
    first=jnp.sum(jnp.where(pad_to(ids,RUNS,-1)[None,:]==run[:,None],OPCAP*run[None,:],0),axis=1)
    return jnp.where(run<NOPS,first,OPCAP*run)
def exchange(x):
    return lax.all_to_all(x.reshape(128,24,128),AXES,split_axis=0,concat_axis=0,tiled=True).reshape(3072,128)
def shards(leaves, coarse_local, m2m, m2l, c2e, l2l, send_box, pair_box, pair_partner, pair_op):
    width=152; box_count=64; edge=EDGE
    ops=operators(jnp.transpose(m2l,(1,2,0)))
    front_sum,own_sum=gather_children(leaves.T,m2m)
    arrived=shifted(front_sum,-1)
    places=run_places(pair_op.reshape(NOPS,OPCAP)[:,0])
    partner=pad_to(2*jnp.where(pair_partner>=0,pair_partner,2624),SLOTS,2*2624)
    box=pad_to(2*pair_box,SLOTS,0)
    arrived,ops=lax.optimization_barrier((arrived,ops))
    packed,up,index=pack_sends(send_box,own_sum,arrived)
    came=exchange(packed)
    local,to_owners=backward(places,box,partner,up,ops)
    returned=exchange(to_owners)
    own=forward(places,partner,box,up,came,ops)
    parent,edges=finish(index,returned,local,own,c2e,coarse_local)
    earlier=shifted(edges,1)
    head=jnp.einsum("pj,oji->poi",earlier,l2l,preferred_element_type=f32).reshape(8*edge,width)
    own_part=jnp.einsum("pj,oji->poi",parent,l2l,preferred_element_type=f32).reshape(8*box_count,width)
    leaf_local=jnp.concatenate([head[8*edge-LEAD:],own_part[:8*box_count-LEAD]])
    return (parent,leaf_local)


def solution(mesh):
    split = P(("slab", "sub"), None)
    flat = P(("slab", "sub"))
    return jax.shard_map(
        shards,
        mesh=mesh,
        in_specs=(split, split, P(), P(), P(), P(), split, flat, flat, flat),
        out_specs=(split, split),
        check_vma=False,
    )
```

```python
import functools

import jax
import jax.numpy as jnp
import numpy as np
from jax import lax
from jax.experimental import pallas as pl
from jax.experimental.pallas import tpu as pltpu
from jax.sharding import PartitionSpec as P
f32=jnp.float32; bf16=jnp.bfloat16
NOPS=316; CAP=20; LEAD=300; OPCAP=13
RUNS=320; SLOTS=4160; COLS=4224; GROUP=32
def pack_maps():
    row=np.arange(192)[:,None]; col=np.arange(160)[None,:]
    same=row//24==col//20
    main=same&(row%24==col%20)
    tail=same&(row%24==20+col%20//5)
    lane=np.arange(128)
    mask=(lane[None,:]//24==np.arange(160)[:,None]%5)
    fold=(lane[:,None]%24==lane[None,:])&(lane[:,None]<120)&(lane[None,:]<24)
    return main,tail,mask,fold
NACC=4
CHUNK=64
def fetch_operators(ta_ref,tb_ref,t_buf,sems):
    copies=[]
    for q in range(5):
        n=min(CHUNK,NOPS-q*CHUNK)
        source=ta_ref.at[pl.ds(q*CHUNK,n)] if q<4 else tb_ref
        copies.append(pltpu.make_async_copy(source,t_buf.at[pl.ds(q*CHUNK,n)],sems.at[q]))
        copies[-1].start()
    return copies
def translate_runs(places,src,dst,flip,copies,table,t_buf,xs,ys,accs):
    def group(g,_):
        for u in range(GROUP):
            k=g*GROUP+u
            first=places[NOPS-1-k if flip else k] if u<GROUP-4 else places[jnp.where(k<NOPS,NOPS-1-k,k) if flip else k]
            for c in range(OPCAP):
                i=pl.multiple_of(src[first+c],2)
                xs[u,2*c:2*c+2,:]=table[pl.ds(i,2),:]
            main=xs[u,pl.ds(0,16,stride=2),:]
            tail=xs[u,pl.ds(1,16,stride=2),:]
            x=jnp.concatenate([main,tail[:,:24]],axis=1).astype(bf16)
            y=jnp.dot(x,t_buf[jnp.minimum(k,NOPS-1)],preferred_element_type=f32)
            ys[u,pl.ds(0,16,stride=2),:]=y[:,:128]
            ys[u,pl.ds(1,16,stride=2),0:24]=y[:,128:]
            for c in range(OPCAP):
                d=pl.multiple_of(dst[first+c],2)
                acc=accs[(u*OPCAP+c)%NACC]
                acc[pl.ds(d,2),:]=acc[pl.ds(d,2),:]+ys[u,2*c:2*c+2,:]
        return 0
    for q in range(5):
        copies[q].wait()
        lax.fori_loop(q*CHUNK//GROUP,(q+1)*CHUNK//GROUP,group,0)
def zero_fill(ref):
    n=ref.shape[0]
    def fill(i,_):
        ref[pl.ds(pl.multiple_of(i*64,64),64),:]=jnp.zeros((64,128),f32)
        return 0
    lax.fori_loop(0,n//64,fill,0,unroll=4)
def sum_rows(accs,first,n):
    main=accs[0][pl.ds(first,n,stride=2),:]
    tail=accs[0][pl.ds(first+1,n,stride=2),:]
    for acc in accs[1:]:
        main=main+acc[pl.ds(first,n,stride=2),:]
        tail=tail+acc[pl.ds(first+1,n,stride=2),:]
    lane=lax.broadcasted_iota(jnp.int32,tail.shape,1)
    return main,jnp.where(lane<24,tail,0.0)
def store_rows(table,first,main,tail):
    n=main.shape[0]
    table[pl.ds(first,n,stride=2),:]=main
    table[pl.ds(first+1,n,stride=2),:]=tail
def widen(rows):
    up=rows.astype(f32)
    return up[:,:128],jnp.concatenate([up[:,128:],jnp.zeros((up.shape[0],104),f32)],axis=1)
def backward_kernel(places,src,dst,up_ref,pm_ref,pt_ref,mask_ref,rep_ref,ta_ref,tb_ref,local_ref,out_ref,t_buf,sems,table,xs,ys,*accs):
    copies=fetch_operators(ta_ref,tb_ref,t_buf,sems)
    xs[...]=jnp.zeros_like(xs)
    ys[...]=jnp.zeros_like(ys)
    for acc in accs:
        zero_fill(acc)
    m,t=widen(up_ref[...])
    store_rows(table,0,m,t)
    translate_runs(places,src,dst,True,copies,table,t_buf,xs,ys,accs)
    m,t=sum_rows(accs,0,64)
    local_ref[:,:128]=m
    local_ref[:,128:]=t[:,:24]
    def step(g,_):
        main,tail=sum_rows(accs,128+320*g,160)
        tail=(jnp.dot(tail.astype(bf16),rep_ref[...],preferred_element_type=f32)*mask_ref[...]).astype(bf16)
        packed=jnp.dot(pm_ref[...],main.astype(bf16),preferred_element_type=f32)+jnp.dot(pt_ref[...],tail,preferred_element_type=f32)
        out_ref[pl.ds(pl.multiple_of(192*g,192),192),:]=packed.astype(bf16)
        return 0
    lax.fori_loop(0,16,step,0,unroll=2)
def forward_kernel(places,src,dst,up_ref,came_ref,pm_ref,pt_ref,mask_ref,fold_ref,ta_ref,tb_ref,own_ref,t_buf,sems,table,xs,ys,*accs):
    copies=fetch_operators(ta_ref,tb_ref,t_buf,sems)
    xs[...]=jnp.zeros_like(xs)
    ys[...]=jnp.zeros_like(ys)
    for acc in accs:
        acc[...]=jnp.zeros_like(acc)
    m,t=widen(up_ref[...])
    store_rows(table,0,m,t)
    table[5248:5264,:]=jnp.zeros((16,128),f32)
    def unpack(g,_):
        rows=came_ref[pl.ds(pl.multiple_of(192*g,192),192),:]
        main=jnp.dot(pm_ref[...],rows,preferred_element_type=f32)
        tail=(jnp.dot(pt_ref[...],rows,preferred_element_type=f32)*mask_ref[...]).astype(bf16)
        tail=jnp.dot(tail,fold_ref[...],preferred_element_type=f32)
        store_rows(table,128+320*g,main,tail)
        return 0
    lax.fori_loop(0,16,unpack,0,unroll=4)
    translate_runs(places,src,dst,False,copies,table,t_buf,xs,ys,accs)
    m,t=sum_rows(accs,0,64)
    own_ref[:,:128]=m
    own_ref[:,128:]=t[:,:24]
SM=pl.BlockSpec(memory_space=pltpu.SMEM); VM=pl.BlockSpec(memory_space=pltpu.VMEM)
def scratch(rows,acc_rows):
    return [pltpu.VMEM((NOPS,152,152),bf16),pltpu.SemaphoreType.DMA((5,)),pltpu.VMEM((rows,128),f32),pltpu.VMEM((GROUP,32,128),f32),pltpu.VMEM((GROUP,32,128),f32)]+[pltpu.VMEM((acc_rows,128),f32)]*NACC
LIM=46*1024*1024
ANY=pl.BlockSpec(memory_space=pltpu.HBM)
def backward(places,src,dst,up,ta,tb):
    main,tail,mask,fold=pack_maps()
    c=lambda a,d: jnp.asarray(a.astype(np.float32),d)
    return pl.pallas_call(backward_kernel,in_specs=[SM]*3+[VM]*5+[ANY]*2,out_specs=[VM,VM],
        out_shape=[jax.ShapeDtypeStruct((64,152),f32),jax.ShapeDtypeStruct((3072,128),bf16)],
        scratch_shapes=scratch(128,5312),compiler_params=pltpu.CompilerParams(vmem_limit_bytes=LIM),name="backward")(
        places,src,dst,up,c(main,bf16),c(tail,bf16),c(mask,f32),c(fold.T,bf16),ta,tb)
def forward(places,src,dst,up,came,ta,tb):
    main,tail,mask,fold=pack_maps()
    c=lambda a,d: jnp.asarray(a.astype(np.float32),d)
    return pl.pallas_call(forward_kernel,in_specs=[SM]*3+[VM]*6+[ANY]*2,out_specs=VM,
        out_shape=jax.ShapeDtypeStruct((64,152),f32),
        scratch_shapes=scratch(5264,128),compiler_params=pltpu.CompilerParams(vmem_limit_bytes=LIM),name="forward")(
        places,src,dst,up,came,c(main.T,bf16),c(tail.T,bf16),c(mask,f32),c(fold,bf16),ta,tb)
def operator_kernel(n,m_ref,t_ref,s1,s2):
    part=pl.program_id(1)
    w=min(128,n+4)
    eye=(lax.broadcasted_iota(jnp.int32,(w,w),0)==lax.broadcasted_iota(jnp.int32,(w,w),1)).astype(bf16)
    def turn(g,_):
        for u in range(19):
            j=19*g+u
            if u%3==2:
                t=lax.dot_general(eye,m_ref[j,:,0:w],(((1,),(1,)),((),())),preferred_element_type=f32)
            else:
                t=m_ref[j,:,0:w].T.astype(f32)
            s1[pl.ds(part*76+j,w,stride=153),:]=t[:,:128]
            s2[pl.ds(part*76+j,w,stride=153),0:24]=t[:,128:]
        return 0
    lax.fori_loop(0,4,turn,0)
    @pl.when(part==1)
    def _():
        def collect(q,_):
            for u in range(4):
                k=4*q+u
                t_ref[k,:,0:128]=s1[pl.ds(k*153,152),:].astype(bf16)
                t_ref[k,:,128:152]=s2[pl.ds(k*153,152),:][:,:24].astype(bf16)
            return 0
        lax.fori_loop(0,n//4,collect,0)
HEAD=256
def operators(m,first,count,n):
    return pl.pallas_call(functools.partial(operator_kernel,n),grid=(count,2),
      in_specs=[pl.BlockSpec((76,152,128),lambda i,j:(j,0,i+first))],
      out_specs=pl.BlockSpec((n,152,152),lambda i,j:(i,0,0)),out_shape=jax.ShapeDtypeStruct((count*n,152,152),bf16),
      scratch_shapes=[pltpu.VMEM((128*153,128),f32)]*2,
      compiler_params=pltpu.CompilerParams(vmem_limit_bytes=50*1024*1024),name="operators")(m)

EDGE=38
def gather_kernel(leaf_ref,m2m_ref,front_ref,own_ref):
    rows=leaf_ref[...].astype(f32).T.astype(bf16)
    box=lax.broadcasted_iota(jnp.int32,(72,512),0)
    row=lax.broadcasted_iota(jnp.int32,(72,512),1)
    total=jnp.zeros((72,152),f32)
    for c in range(8):
        hot=jnp.where(row==8*box+(c-4),1.0,0.0).astype(bf16)
        child=jnp.dot(hot,rows,preferred_element_type=f32).astype(bf16)
        total=total+jnp.dot(child,m2m_ref[c],preferred_element_type=f32)
    front_ref[...]=total[:EDGE]
    own_ref[...]=jnp.concatenate([total[EDGE:65],jnp.zeros((37,152),f32)],axis=0)
def gather_children(leaf_t,m2m):
    return pl.pallas_call(gather_kernel,in_specs=[VM]*2,out_specs=[VM]*2,
        out_shape=[jax.ShapeDtypeStruct((EDGE,152),f32),jax.ShapeDtypeStruct((64,152),f32)],
        compiler_params=pltpu.CompilerParams(vmem_limit_bytes=16*1024*1024),name="gather")(leaf_t,m2m)
def slot_hot(index_ref,g):
    boxes=lax.broadcasted_iota(jnp.int32,(64,192),0).astype(f32)+1.0
    return jnp.concatenate([jnp.where(boxes==index_ref[16*b+g:16*b+g+1,:],1.0,0.0).astype(bf16) for b in range(6)],axis=0)
def send_kernel(send_ref,own_ref,arrived_ref,pm_ref,pt_ref,rep_ref,out_ref,up_ref,index_ref):
    plus=(send_ref[...]+1).astype(f32)
    plus=jnp.concatenate([plus[:,160*g:160*g+160] for g in range(16)],axis=0)
    slot=lax.rem(lax.broadcasted_iota(jnp.int32,(16,160),1),5)
    index_ref[0:16,:]=jnp.dot(plus.astype(bf16),pm_ref[...],preferred_element_type=f32)
    for t in range(5):
        index_ref[16*t+16:16*t+32,:]=jnp.dot(jnp.where(slot==t,plus,0.0).astype(bf16),pt_ref[...],preferred_element_type=f32)
    up=(own_ref[...]+jnp.concatenate([jnp.zeros((64-EDGE,152),f32),arrived_ref[...]],axis=0)).astype(bf16)
    up_ref[...]=up
    tail=jnp.dot(jnp.concatenate([up[:,128:],jnp.zeros((64,104),bf16)],axis=1),rep_ref[...],preferred_element_type=f32)
    lane=lax.broadcasted_iota(jnp.int32,(64,128),1)
    values=jnp.concatenate([up[:,:128]]+[jnp.where((lane>=24*t)&(lane<24*t+24),tail,0.0).astype(bf16) for t in range(5)],axis=0)
    for g in range(16):
        out_ref[192*g:192*g+192,:]=lax.dot_general(slot_hot(index_ref,g),values,(((0,),(0,)),((),())),preferred_element_type=f32).astype(bf16)
def pack_sends(send,own,arrived):
    main,tail,mask,fold=pack_maps()
    c=lambda a: jnp.asarray(a.astype(np.float32),bf16)
    return pl.pallas_call(send_kernel,in_specs=[VM]*6,out_specs=[VM]*3,
        out_shape=[jax.ShapeDtypeStruct((3072,128),bf16),jax.ShapeDtypeStruct((64,152),bf16),jax.ShapeDtypeStruct((96,192),f32)],
        compiler_params=pltpu.CompilerParams(vmem_limit_bytes=16*1024*1024),name="send")(send,own,arrived,c(main.T),c(tail.T),c(fold.T))
def finish_kernel(index_ref,came_ref,local_ref,own_ref,c2e_ref,coarse_ref,parent_ref,edge_ref):
    got=jnp.zeros((384,128),f32)
    for g in range(16):
        got=got+jnp.dot(slot_hot(index_ref,g),came_ref[192*g:192*g+192,:],preferred_element_type=f32)
    tail=got[64:128,0:24]
    for t in range(1,5):
        tail=tail+got[64+64*t:128+64*t,24*t:24*t+24]
    check=local_ref[...]+own_ref[...]+jnp.concatenate([got[:64],tail],axis=1)
    parent=(jnp.dot(check,c2e_ref[...],precision=lax.Precision.HIGHEST,preferred_element_type=f32)+coarse_ref[...].astype(f32)).astype(bf16)
    parent_ref[...]=parent
    edge_ref[...]=parent[64-EDGE:]
def finish(index,came,local,own,c2e,coarse):
    return pl.pallas_call(finish_kernel,in_specs=[VM]*6,out_specs=[VM]*2,
        out_shape=[jax.ShapeDtypeStruct((64,152),bf16),jax.ShapeDtypeStruct((EDGE,152),bf16)],
        compiler_params=pltpu.CompilerParams(vmem_limit_bytes=16*1024*1024),name="finish")(index,came,local,own,c2e,coarse)
def pad_to(a,n,v):
    return jnp.concatenate([a,jnp.full((n-a.shape[0],),v,a.dtype)])
AXES=("slab","sub")
def shifted(x, by):
    count = lax.axis_size(AXES)
    return lax.ppermute(x, AXES, [(i, (i + by) % count) for i in range(count)])
def run_places(ids):
    run=jnp.arange(RUNS,dtype=jnp.int32)
    first=jnp.sum(jnp.where(pad_to(ids,RUNS,-1)[None,:]==run[:,None],OPCAP*run[None,:],0),axis=1)
    return jnp.where(run<NOPS,first,OPCAP*run)
def exchange(x):
    return lax.all_to_all(x.reshape(128,24,128),AXES,split_axis=0,concat_axis=0,tiled=True).reshape(3072,128)
def shards(leaves, coarse_local, m2m, m2l, c2e, l2l, send_box, pair_box, pair_partner, pair_op):
    width=152; box_count=64; edge=EDGE
    m2l_t=jnp.transpose(m2l,(1,2,0))
    ops_a=operators(m2l_t,0,2,128)
    leaves_t,m2m,ops_a=lax.optimization_barrier((leaves.T,m2m,ops_a))
    front_sum,own_sum=gather_children(leaves_t,m2m)
    arrived=shifted(front_sum,-1)
    front_sum,own_sum,m2l_t=lax.optimization_barrier((front_sum,own_sum,m2l_t))
    ops_b=operators(m2l_t,2,1,60)
    places=run_places(pair_op.reshape(NOPS,OPCAP)[:,0])
    partner=pad_to(2*jnp.where(pair_partner>=0,pair_partner,2624),SLOTS,2*2624)
    box=pad_to(2*pair_box,SLOTS,0)
    arrived,ops_b=lax.optimization_barrier((arrived,ops_b))
    packed,up,index=pack_sends(send_box,own_sum,arrived)
    came=exchange(packed)
    local,to_owners=backward(places,box,partner,up,ops_a,ops_b)
    returned=exchange(to_owners)
    own=forward(places,partner,box,up,came,ops_a,ops_b)
    parent,edges=finish(index,returned,local,own,c2e,coarse_local)
    earlier=shifted(edges,1)
    head=jnp.einsum("pj,oji->poi",earlier,l2l,preferred_element_type=f32).reshape(8*edge,width)
    own_part=jnp.einsum("pj,oji->poi",parent,l2l,preferred_element_type=f32).reshape(8*box_count,width)
    leaf_local=jnp.concatenate([head[8*edge-LEAD:],own_part[:8*box_count-LEAD]])
    return (parent,leaf_local)


def solution(mesh):
    split = P(("slab", "sub"), None)
    flat = P(("slab", "sub"))
    return jax.shard_map(
        shards,
        mesh=mesh,
        in_specs=(split, split, P(), P(), P(), P(), split, flat, flat, flat),
        out_specs=(split, split),
        check_vma=False,
    )
```

```python
import functools

import jax
import jax.numpy as jnp
import numpy as np
from jax import lax
from jax.experimental import pallas as pl
from jax.experimental.pallas import tpu as pltpu
from jax.sharding import PartitionSpec as P
f32=jnp.float32; bf16=jnp.bfloat16
NOPS=316; CAP=20; LEAD=300; OPCAP=13
RUNS=320; SLOTS=4160; COLS=4224; GROUP=64
def pack_maps():
    row=np.arange(192)[:,None]; col=np.arange(160)[None,:]
    same=row//24==col//20
    main=same&(row%24==col%20)
    tail=same&(row%24==20+col%20//5)
    lane=np.arange(128)
    mask=(lane[None,:]//24==np.arange(160)[:,None]%5)
    fold=(lane[:,None]%24==lane[None,:])&(lane[:,None]<120)&(lane[None,:]<24)
    return main,tail,mask,fold
NACC=4
CHUNK=64
def fetch_operators(t_ref,t_buf,sems):
    copies=[]
    for q in range(5):
        n=min(CHUNK,NOPS-q*CHUNK)
        copies.append(pltpu.make_async_copy(t_ref.at[pl.ds(q*CHUNK,n)],t_buf.at[pl.ds(q*CHUNK,n)],sems.at[q]))
        copies[-1].start()
    return copies
def translate_runs(places,src,dst,flip,copies,table,t_buf,xs,ys,accs):
    def group(g,_):
        for u in range(GROUP):
            k=g*GROUP+u
            first=places[NOPS-1-k if flip else k] if u<GROUP-4 else places[jnp.where(k<NOPS,NOPS-1-k,k) if flip else k]
            for c in range(OPCAP):
                i=pl.multiple_of(src[first+c],2)
                xs[u,2*c:2*c+2,:]=table[pl.ds(i,2),:]
            main=xs[u,pl.ds(0,16,stride=2),:]
            tail=xs[u,pl.ds(1,16,stride=2),:]
            x=jnp.concatenate([main,tail[:,:24]],axis=1).astype(bf16)
            y=jnp.dot(x,t_buf[jnp.minimum(k,NOPS-1)],preferred_element_type=f32)
            ys[u,pl.ds(0,16,stride=2),:]=y[:,:128]
            ys[u,pl.ds(1,16,stride=2),0:24]=y[:,128:]
            for c in range(OPCAP):
                d=pl.multiple_of(dst[first+c],2)
                acc=accs[(u*OPCAP+c)%NACC]
                acc[pl.ds(d,2),:]=acc[pl.ds(d,2),:]+ys[u,2*c:2*c+2,:]
        return 0
    for q in range(5):
        copies[q].wait()
        lax.fori_loop(q*CHUNK//GROUP,(q+1)*CHUNK//GROUP,group,0)
def zero_fill(ref):
    n=ref.shape[0]
    def fill(i,_):
        ref[pl.ds(pl.multiple_of(i*64,64),64),:]=jnp.zeros((64,128),f32)
        return 0
    lax.fori_loop(0,n//64,fill,0,unroll=4)
def sum_rows(accs,first,n):
    main=accs[0][pl.ds(first,n,stride=2),:]
    tail=accs[0][pl.ds(first+1,n,stride=2),:]
    for acc in accs[1:]:
        main=main+acc[pl.ds(first,n,stride=2),:]
        tail=tail+acc[pl.ds(first+1,n,stride=2),:]
    lane=lax.broadcasted_iota(jnp.int32,tail.shape,1)
    return main,jnp.where(lane<24,tail,0.0)
def store_rows(table,first,main,tail):
    n=main.shape[0]
    table[pl.ds(first,n,stride=2),:]=main
    table[pl.ds(first+1,n,stride=2),:]=tail
def widen(rows):
    up=rows.astype(f32)
    return up[:,:128],jnp.concatenate([up[:,128:],jnp.zeros((up.shape[0],104),f32)],axis=1)
def backward_kernel(places,src,dst,up_ref,pm_ref,pt_ref,mask_ref,rep_ref,t_ref,local_ref,out_ref,t_buf,sems,table,xs,ys,*accs):
    copies=fetch_operators(t_ref,t_buf,sems)
    xs[...]=jnp.zeros_like(xs)
    ys[...]=jnp.zeros_like(ys)
    for acc in accs:
        zero_fill(acc)
    m,t=widen(up_ref[...])
    store_rows(table,0,m,t)
    translate_runs(places,src,dst,True,copies,table,t_buf,xs,ys,accs)
    m,t=sum_rows(accs,0,64)
    local_ref[:,:128]=m
    local_ref[:,128:]=t[:,:24]
    def step(g,_):
        main,tail=sum_rows(accs,128+320*g,160)
        tail=(jnp.dot(tail.astype(bf16),rep_ref[...],preferred_element_type=f32)*mask_ref[...]).astype(bf16)
        packed=jnp.dot(pm_ref[...],main.astype(bf16),preferred_element_type=f32)+jnp.dot(pt_ref[...],tail,preferred_element_type=f32)
        out_ref[pl.ds(pl.multiple_of(192*g,192),192),:]=packed.astype(bf16)
        return 0
    lax.fori_loop(0,16,step,0,unroll=8)
def forward_kernel(places,src,dst,up_ref,came_ref,pm_ref,pt_ref,mask_ref,fold_ref,t_ref,own_ref,t_buf,sems,table,xs,ys,*accs):
    copies=fetch_operators(t_ref,t_buf,sems)
    xs[...]=jnp.zeros_like(xs)
    ys[...]=jnp.zeros_like(ys)
    for acc in accs:
        acc[...]=jnp.zeros_like(acc)
    m,t=widen(up_ref[...])
    store_rows(table,0,m,t)
    table[5248:5264,:]=jnp.zeros((16,128),f32)
    def unpack(g,_):
        rows=came_ref[pl.ds(pl.multiple_of(192*g,192),192),:]
        main=jnp.dot(pm_ref[...],rows,preferred_element_type=f32)
        tail=(jnp.dot(pt_ref[...],rows,preferred_element_type=f32)*mask_ref[...]).astype(bf16)
        tail=jnp.dot(tail,fold_ref[...],preferred_element_type=f32)
        store_rows(table,128+320*g,main,tail)
        return 0
    lax.fori_loop(0,16,unpack,0,unroll=8)
    translate_runs(places,src,dst,False,copies,table,t_buf,xs,ys,accs)
    m,t=sum_rows(accs,0,64)
    own_ref[:,:128]=m
    own_ref[:,128:]=t[:,:24]
SM=pl.BlockSpec(memory_space=pltpu.SMEM); VM=pl.BlockSpec(memory_space=pltpu.VMEM)
def scratch(rows,acc_rows):
    return [pltpu.VMEM((NOPS,152,152),bf16),pltpu.SemaphoreType.DMA((5,)),pltpu.VMEM((rows,128),f32),pltpu.VMEM((GROUP,32,128),f32),pltpu.VMEM((GROUP,32,128),f32)]+[pltpu.VMEM((acc_rows,128),f32)]*NACC
LIM=46*1024*1024
ANY=pl.BlockSpec(memory_space=pl.ANY)
def backward(places,src,dst,up,t):
    main,tail,mask,fold=pack_maps()
    c=lambda a,d: jnp.asarray(a.astype(np.float32),d)
    return pl.pallas_call(backward_kernel,in_specs=[SM]*3+[VM]*5+[ANY],out_specs=[VM,VM],
        out_shape=[jax.ShapeDtypeStruct((64,152),f32),jax.ShapeDtypeStruct((3072,128),bf16)],
        scratch_shapes=scratch(128,5312),compiler_params=pltpu.CompilerParams(vmem_limit_bytes=LIM),name="backward")(
        places,src,dst,up,c(main,bf16),c(tail,bf16),c(mask,f32),c(fold.T,bf16),t)
def forward(places,src,dst,up,came,t):
    main,tail,mask,fold=pack_maps()
    c=lambda a,d: jnp.asarray(a.astype(np.float32),d)
    return pl.pallas_call(forward_kernel,in_specs=[SM]*3+[VM]*6+[ANY],out_specs=VM,
        out_shape=jax.ShapeDtypeStruct((64,152),f32),
        scratch_shapes=scratch(5264,128),compiler_params=pltpu.CompilerParams(vmem_limit_bytes=LIM),name="forward")(
        places,src,dst,up,came,c(main.T,bf16),c(tail.T,bf16),c(mask,f32),c(fold,bf16),t)
def operator_kernel(m_ref,t_ref,s1,s2):
    block=pl.program_id(0); part=pl.program_id(1)
    def turn(n):
        eye=(lax.broadcasted_iota(jnp.int32,(n,n),0)==lax.broadcasted_iota(jnp.int32,(n,n),1)).astype(bf16)
        def body(g,_):
            for u in range(19):
                j=19*g+u
                if u%3==2:
                    t=lax.dot_general(eye,m_ref[j,:,0:n],(((1,),(1,)),((),())),preferred_element_type=f32)
                else:
                    t=m_ref[j,:,0:n].T.astype(f32)
                s1[pl.ds(part*76+j,n,stride=153),:]=t[:,:128]
                s2[pl.ds(part*76+j,n,stride=153),0:24]=t[:,128:]
            return 0
        lax.fori_loop(0,4,body,0)
    def collect(n):
        def body(q,_):
            for u in range(4):
                k=4*q+u
                t_ref[k,:,0:128]=s1[pl.ds(k*153,152),:].astype(bf16)
                t_ref[k,:,128:152]=s2[pl.ds(k*153,152),:][:,:24].astype(bf16)
            return 0
        lax.fori_loop(0,n//4,body,0)
    @pl.when(block<2)
    def _():
        turn(128)
    @pl.when(block==2)
    def _():
        turn(64)
    @pl.when((part==1)&(block<2))
    def _():
        collect(128)
    @pl.when((part==1)&(block==2))
    def _():
        collect(60)
def operators(m):
    return pl.pallas_call(operator_kernel,grid=(3,2),in_specs=[pl.BlockSpec((76,152,128),lambda i,j:(j,0,i))],
      out_specs=pl.BlockSpec((128,152,152),lambda i,j:(i,0,0)),out_shape=jax.ShapeDtypeStruct((NOPS,152,152),bf16),
      scratch_shapes=[pltpu.VMEM((128*153,128),f32)]*2,
      compiler_params=pltpu.CompilerParams(vmem_limit_bytes=50*1024*1024),name="operators")(m)

EDGE=38
def gather_kernel(leaf_ref,m2m_ref,front_ref,own_ref):
    rows=leaf_ref[...].astype(f32).T.astype(bf16)
    box=lax.broadcasted_iota(jnp.int32,(72,512),0)
    row=lax.broadcasted_iota(jnp.int32,(72,512),1)
    total=jnp.zeros((72,152),f32)
    for c in range(8):
        hot=jnp.where(row==8*box+(c-4),1.0,0.0).astype(bf16)
        child=jnp.dot(hot,rows,preferred_element_type=f32).astype(bf16)
        total=total+jnp.dot(child,m2m_ref[c],preferred_element_type=f32)
    front_ref[...]=total[:EDGE]
    own_ref[...]=jnp.concatenate([total[EDGE:65],jnp.zeros((37,152),f32)],axis=0)
def gather_children(leaf_t,m2m):
    return pl.pallas_call(gather_kernel,in_specs=[VM]*2,out_specs=[VM]*2,
        out_shape=[jax.ShapeDtypeStruct((EDGE,152),f32),jax.ShapeDtypeStruct((64,152),f32)],
        compiler_params=pltpu.CompilerParams(vmem_limit_bytes=16*1024*1024),name="gather")(leaf_t,m2m)
def slot_hot(index_ref,g):
    boxes=lax.broadcasted_iota(jnp.int32,(64,192),0).astype(f32)+1.0
    return jnp.concatenate([jnp.where(boxes==index_ref[16*b+g:16*b+g+1,:],1.0,0.0).astype(bf16) for b in range(6)],axis=0)
def send_kernel(send_ref,own_ref,arrived_ref,pm_ref,pt_ref,rep_ref,out_ref,up_ref,index_ref):
    plus=(send_ref[...]+1).astype(f32)
    plus=jnp.concatenate([plus[:,160*g:160*g+160] for g in range(16)],axis=0)
    slot=lax.rem(lax.broadcasted_iota(jnp.int32,(16,160),1),5)
    index_ref[0:16,:]=jnp.dot(plus.astype(bf16),pm_ref[...],preferred_element_type=f32)
    for t in range(5):
        index_ref[16*t+16:16*t+32,:]=jnp.dot(jnp.where(slot==t,plus,0.0).astype(bf16),pt_ref[...],preferred_element_type=f32)
    up=(own_ref[...]+jnp.concatenate([jnp.zeros((64-EDGE,152),f32),arrived_ref[...]],axis=0)).astype(bf16)
    up_ref[...]=up
    tail=jnp.dot(jnp.concatenate([up[:,128:],jnp.zeros((64,104),bf16)],axis=1),rep_ref[...],preferred_element_type=f32)
    lane=lax.broadcasted_iota(jnp.int32,(64,128),1)
    values=jnp.concatenate([up[:,:128]]+[jnp.where((lane>=24*t)&(lane<24*t+24),tail,0.0).astype(bf16) for t in range(5)],axis=0)
    for g in range(16):
        out_ref[192*g:192*g+192,:]=lax.dot_general(slot_hot(index_ref,g),values,(((0,),(0,)),((),())),preferred_element_type=f32).astype(bf16)
def pack_sends(send,own,arrived):
    main,tail,mask,fold=pack_maps()
    c=lambda a: jnp.asarray(a.astype(np.float32),bf16)
    return pl.pallas_call(send_kernel,in_specs=[VM]*6,out_specs=[VM]*3,
        out_shape=[jax.ShapeDtypeStruct((3072,128),bf16),jax.ShapeDtypeStruct((64,152),bf16),jax.ShapeDtypeStruct((96,192),f32)],
        compiler_params=pltpu.CompilerParams(vmem_limit_bytes=16*1024*1024),name="send")(send,own,arrived,c(main.T),c(tail.T),c(fold.T))
def finish_kernel(index_ref,came_ref,local_ref,own_ref,c2e_ref,coarse_ref,parent_ref,edge_ref):
    got=jnp.zeros((384,128),f32)
    for g in range(16):
        got=got+jnp.dot(slot_hot(index_ref,g),came_ref[192*g:192*g+192,:],preferred_element_type=f32)
    tail=got[64:128,0:24]
    for t in range(1,5):
        tail=tail+got[64+64*t:128+64*t,24*t:24*t+24]
    check=local_ref[...]+own_ref[...]+jnp.concatenate([got[:64],tail],axis=1)
    parent=(jnp.dot(check,c2e_ref[...],precision=lax.Precision.HIGHEST,preferred_element_type=f32)+coarse_ref[...].astype(f32)).astype(bf16)
    parent_ref[...]=parent
    edge_ref[...]=parent[64-EDGE:]
def finish(index,came,local,own,c2e,coarse):
    return pl.pallas_call(finish_kernel,in_specs=[VM]*6,out_specs=[VM]*2,
        out_shape=[jax.ShapeDtypeStruct((64,152),bf16),jax.ShapeDtypeStruct((EDGE,152),bf16)],
        compiler_params=pltpu.CompilerParams(vmem_limit_bytes=16*1024*1024),name="finish")(index,came,local,own,c2e,coarse)
def pad_to(a,n,v):
    return jnp.concatenate([a,jnp.full((n-a.shape[0],),v,a.dtype)])
AXES=("slab","sub")
def shifted(x, by):
    count = lax.axis_size(AXES)
    return lax.ppermute(x, AXES, [(i, (i + by) % count) for i in range(count)])
def run_places(ids):
    run=jnp.arange(RUNS,dtype=jnp.int32)
    first=jnp.sum(jnp.where(pad_to(ids,RUNS,-1)[None,:]==run[:,None],OPCAP*run[None,:],0),axis=1)
    return jnp.where(run<NOPS,first,OPCAP*run)
def exchange(x):
    return lax.all_to_all(x.reshape(128,24,128),AXES,split_axis=0,concat_axis=0,tiled=True).reshape(3072,128)
def shards(leaves, coarse_local, m2m, m2l, c2e, l2l, send_box, pair_box, pair_partner, pair_op):
    width=152; box_count=64; edge=EDGE
    ops=operators(jnp.transpose(m2l,(1,2,0)))
    front_sum,own_sum=gather_children(leaves.T,m2m)
    arrived=shifted(front_sum,-1)
    places=run_places(pair_op.reshape(NOPS,OPCAP)[:,0])
    partner=pad_to(2*jnp.where(pair_partner>=0,pair_partner,2624),SLOTS,2*2624)
    box=pad_to(2*pair_box,SLOTS,0)
    arrived,ops=lax.optimization_barrier((arrived,ops))
    packed,up,index=pack_sends(send_box,own_sum,arrived)
    came=exchange(packed)
    local,to_owners=backward(places,box,partner,up,ops)
    returned=exchange(to_owners)
    own=forward(places,partner,box,up,came,ops)
    parent,edges=finish(index,returned,local,own,c2e,coarse_local)
    earlier=shifted(edges,1)
    head=jnp.einsum("pj,oji->poi",earlier,l2l,preferred_element_type=f32).reshape(8*edge,width)
    own_part=jnp.einsum("pj,oji->poi",parent,l2l,preferred_element_type=f32).reshape(8*box_count,width)
    leaf_local=jnp.concatenate([head[8*edge-LEAD:],own_part[:8*box_count-LEAD]])
    return (parent,leaf_local)


def solution(mesh):
    split = P(("slab", "sub"), None)
    flat = P(("slab", "sub"))
    return jax.shard_map(
        shards,
        mesh=mesh,
        in_specs=(split, split, P(), P(), P(), P(), split, flat, flat, flat),
        out_specs=(split, split),
        check_vma=False,
    )
```
